256 devices in a mesh: prot: 16 (over y, x_hi, core), var: 8 (over z), samp: 2 (over x_lo).
Axes of the slice: x: 4 (x_hi: 2, x_lo: 2; x = x_hi * 2 + x_lo), y: 4, z: 8, core: 2. Of those that a mesh axis runs over, the one named last changes fastest.
Arguments:
- genotype: bfloat16 [196608, 2048], P(('prot', 'var'), 'samp'), may hold values from 0 to 2
- proteins: bfloat16 [2048, 2944], P('samp', 'prot'), may hold values from -16 to 16
- cis_pick: int32 [128, 16], P(('prot', 'var')), may hold values from -1 to 23, as said below
- perm_table: int32 [4, 2048], P(None, 'samp'), may hold values from 0 to 2047, each once within a row
Outputs:
- trans_score: bfloat16 [196608, 2944], P(('prot', 'var'), 'samp')
- cis_stat: float32 [4, 2944], P(None, 'prot')
The draws below stay inside these ranges and needn't reach their ends.
Inputs may be any that keep to these rules, and one draw needn't show every extreme that they name: `cis_pick`: each entry names one of the 24 cis blocks of its slab, or is -1 for no cis block. `perm_table`: each row holds every sample index once.
All inputs are finite; a program needn't handle non-finite values.
Results may differ from the reference program's by a relative error of at most 0.001.
Values may be sent and summed in bfloat16 or wider, within the bound.
A program may use at most 128 MiB of HBM per device.

```python
import jax
import jax.numpy as jnp
from jax import lax

VAR_DEV = 1536
PROT_BLK = 184
VB = 64
NPERM = 4
VARIANTS = 196608
SAMPLES = 2048
PROTEINS = 2944
SLABS = 128
BLK_DEV = 24
N_PROT = 16
N_VAR = 8


def draw_genotype(key, part):
    key = jax.random.fold_in(key, 11)
    key_scale, key_noise = jax.random.split(key, 2)
    spread = jnp.exp(jax.random.uniform(key_scale, (VARIANTS, 1), jnp.float32, jnp.log(0.1), 0.0))
    noise = jax.random.uniform(key_noise, (VARIANTS, SAMPLES), jnp.float32, -1.0, 1.0)
    values = 1.0 + spread * noise
    return jnp.clip(values, 0.0, 2.0).astype(jnp.bfloat16)


def draw_proteins(key, part):
    key = jax.random.fold_in(key, 23)
    key_scale, key_noise = jax.random.split(key, 2)
    spread = jnp.exp(jax.random.uniform(key_scale, (1, PROTEINS), jnp.float32, jnp.log(0.3), jnp.log(3.0)))
    values = spread * jax.random.normal(key_noise, (SAMPLES, PROTEINS), jnp.float32)
    return jnp.clip(values, -16.0, 16.0).astype(jnp.bfloat16)


def draw_cis_pick(key, part):
    key = jax.random.fold_in(key, 37)
    key_block, key_keep = jax.random.split(key)
    blocks = jax.random.randint(key_block, (SLABS, N_PROT), 0, BLK_DEV, jnp.int32)
    keeper = jax.random.randint(key_keep, (SLABS, N_PROT), 0, 5, jnp.int32) < 3
    picked = jnp.where(keeper, blocks, -1).astype(jnp.int32)
    picked = picked.at[0, 0].set(BLK_DEV - 1)
    picked = picked.at[0, 1].set(-1)
    return picked


def setup_inputs(seed: int = 0) -> dict:
    seeds = jax.random.split(jax.random.key(seed), 5)
    genotype = draw_genotype(jax.random.fold_in(seeds[4], 71), 0)
    proteins = draw_proteins(jax.random.fold_in(seeds[4], 71), 0)
    cis_pick = draw_cis_pick(jax.random.fold_in(seeds[4], 71), 0)
    perm_table = jax.vmap(lambda own: jax.random.permutation(own, SAMPLES))(jax.random.split(seeds[3], NPERM)).reshape((NPERM, SAMPLES)).astype(jnp.int32)
    return dict(genotype=genotype, proteins=proteins, cis_pick=cis_pick, perm_table=perm_table)


epsilon = 1e-06

def reference(genotype, proteins, cis_pick, perm_table):
    count_all = jnp.float32(SAMPLES)
    root_count = jnp.sqrt(count_all)
    prot_wide = proteins.astype(jnp.float32)
    mean_y = lax.optimization_barrier(jnp.sum(prot_wide, 0)) / count_all
    var_y = lax.optimization_barrier(jnp.sum(prot_wide * prot_wide, 0)) / count_all - mean_y * mean_y
    inv_y = lax.rsqrt(var_y + epsilon)

    def trans_slab(slab_rows):
        cross = jnp.dot(slab_rows, proteins, preferred_element_type=jnp.float32)
        widened = slab_rows.astype(jnp.float32)
        mean_g = lax.optimization_barrier(jnp.sum(widened, 1)) / count_all
        var_g = lax.optimization_barrier(jnp.sum(widened * widened, 1)) / count_all - mean_g * mean_g
        covar = cross / count_all - mean_g[:, None] * mean_y[None, :]
        score = root_count * covar * lax.rsqrt(var_g + epsilon)[:, None] * inv_y[None, :]
        return score.astype(jnp.bfloat16)
    slabs = genotype.reshape(SLABS, VAR_DEV, SAMPLES)
    trans_score = lax.map(trans_slab, slabs).reshape(VARIANTS, PROTEINS)
    permuted = jnp.take(proteins, perm_table, axis=0).astype(jnp.float32)
    permuted = permuted.reshape(NPERM, SAMPLES, N_PROT, PROT_BLK)
    mean_block = mean_y.reshape(N_PROT, PROT_BLK)
    inv_block = inv_y.reshape(N_PROT, PROT_BLK)

    def cis_slab(running, pair):
        slab_rows, slab_picks = pair
        blocks = slab_rows.reshape(BLK_DEV, VB, SAMPLES)
        chosen = jnp.take(blocks, jnp.maximum(slab_picks, 0).astype(jnp.int32), axis=0).astype(jnp.float32)
        keep_mask = (slab_picks >= 0).astype(jnp.float32)
        cross = jnp.einsum('qvs,ksqj->kqvj', chosen, permuted)
        mean_g = lax.optimization_barrier(jnp.sum(chosen, 2)) / count_all
        var_g = lax.optimization_barrier(jnp.sum(chosen * chosen, 2)) / count_all - mean_g * mean_g
        covar = cross / count_all - mean_g[None, :, :, None] * mean_block[None, :, None, :]
        score = root_count * covar * lax.rsqrt(var_g + epsilon)[None, :, :, None] * inv_block[None, :, None, :]
        running = running + lax.optimization_barrier(jnp.sum(score * score, 2)) * keep_mask[None, :, None]
        return (running, None)
    start_value = jnp.zeros((NPERM, N_PROT, PROT_BLK), jnp.float32)
    summed, _ = lax.scan(cis_slab, start_value, (slabs, cis_pick))
    cis_stat = summed.reshape(NPERM, PROTEINS) / jnp.float32(VB * N_PROT * N_VAR)
    return (trans_score, cis_stat)
```

```python
import functools

import jax
import jax.numpy as jnp
from jax import lax
from jax.experimental import pallas as pl
from jax.experimental.pallas import tpu as pltpu
from jax.sharding import PartitionSpec as P

MESH = pl.DeviceIdType.MESH
VB = 64
BLOCKS = 24
TILES = BLOCKS // 2
ROWS = VB * BLOCKS
HALF = 1024
ALL = 2 * HALF
PB = 184
COLS = 8 * PB
CHUNKS = (4, 4, 4, 4, 4, 2, 2)
STARTS = tuple(sum(CHUNKS[:c]) for c in range(len(CHUNKS)))
CIS_CHUNKS = 2
GROUPS = ((4, 0, 8), (5, 8, 10), (6, 10, 11), (7, 11, 12))
EPS = 1e-6
N = float(ALL)
MIB = 1 << 20
NT = (((1,), (1,)), ((), ()))


def dot_nt(a, b):
    return lax.dot_general(a, b, NT, preferred_element_type=jnp.float32)


def block_order(pick_ref, first, flag, order):
    picks = [pick_ref[0, first + i] for i in range(8)]
    for b in range(BLOCKS):
        hit = jnp.int32(0)
        for pick in picks:
            hit = hit | (pick == b).astype(jnp.int32)
        flag[b] = hit
    at = jnp.int32(0)
    for rank in range(3):
        for b in range(BLOCKS):
            mine, pair = flag[b], flag[b ^ 1]
            here = (mine, (1 - mine) * pair, (1 - mine) * (1 - pair))[rank]
            order[at] = jnp.int32(b)
            at = at + here


def sort_kernel(pick_ref, g_ref, *refs):
    outs, (flag, order, sems) = refs[:-3], refs[-3:]
    block_order(pick_ref, 8 * (1 - lax.axis_index("samp")), flag, order)
    copies = []
    for c, blocks in enumerate(CHUNKS):
        for t in range(blocks):
            r = STARTS[c] + t
            row = pl.multiple_of(order[r] * VB, VB)
            copy = pltpu.make_async_copy(g_ref.at[pl.ds(row, VB)], outs[c].at[pl.ds(t * VB, VB)], sems.at[r])
            copy.start()
            copies.append(copy)
    for copy in copies:
        copy.wait()


def sort_blocks(pick, genotype):
    return pl.pallas_call(
        sort_kernel,
        out_shape=[jax.ShapeDtypeStruct((b * VB, HALF), jnp.bfloat16) for b in CHUNKS],
        in_specs=[pl.BlockSpec(memory_space=pltpu.SMEM), pl.BlockSpec(memory_space=pltpu.HBM)],
        out_specs=[pl.BlockSpec(memory_space=pltpu.VMEM)] * len(CHUNKS),
        scratch_shapes=[
            pltpu.SMEM((BLOCKS,), jnp.int32),
            pltpu.SMEM((BLOCKS + 8,), jnp.int32),
            pltpu.SemaphoreType.DMA((BLOCKS,)),
        ],
        compiler_params=pltpu.CompilerParams(vmem_limit_bytes=8 * MIB),
        name="sort_blocks",
    )(pick, genotype)


PLAN_TILE, PLAN_PLACE, PLAN_BLOCK, PLAN_KEEP, PLAN = 24, 36, 44, 52, 64


def plan_kernel(pick_ref, plan, flag, order, seen):
    first = 8 * lax.axis_index("samp")
    block_order(pick_ref, first, flag, order)
    for t in range(TILES):
        seen[t] = jnp.int32(0)
    done = jnp.int32(0)
    for r in range(BLOCKS):
        b = order[r]
        plan[b] = jnp.int32(r)
        t = b // 2
        before = seen[t]
        seen[t] = before + 1
        plan[PLAN_TILE + done] = t
        done = done + before
    for i in range(8):
        pick = pick_ref[0, first + i]
        keep = (pick >= 0).astype(jnp.int32)
        block = jnp.maximum(pick, 0)
        plan[PLAN_PLACE + i] = plan[block] * keep
        plan[PLAN_BLOCK + i] = block
        plan[PLAN_KEEP + i] = keep


def make_plan(pick):
    smem = pl.BlockSpec(memory_space=pltpu.SMEM)
    return pl.pallas_call(
        plan_kernel,
        out_shape=jax.ShapeDtypeStruct((PLAN,), jnp.int32),
        in_specs=[smem],
        out_specs=smem,
        scratch_shapes=[pltpu.SMEM((n,), jnp.int32) for n in (BLOCKS, BLOCKS + 8, TILES)],
        name="make_plan",
    )(pick)


def protein_kernel(prot, perm_ref, data, perm_out, s_own, s_perm, rp, s1, r1, s2, r2, sa, ra, sb, rb, s3, r3, sd, rd):
    p, z, s = lax.axis_index("prot"), lax.axis_index("var"), lax.axis_index("samp")
    c, xh, y = p % 2, (p // 2) % 2, p // 4
    half, a = y // 2, (y % 2) * 2 + xh
    away = (s + half) % 2
    gap = a - y
    own = (1 - away) * (1 - (gap * gap + 8) // 9)

    def device(y2, x2):
        return y2 * 4 + x2 * 2 + c

    barrier = pltpu.get_barrier_semaphore()

    def signal(dev):
        pl.semaphore_signal(barrier, inc=1, device_id=dev, device_id_type=MESH)

    source = device(2 * s + y // 2, y % 2)

    @pl.when(own == 0)
    def _():
        signal((source, z, s))

    signal((source, z, 1 - s))
    y_peers = [(device((y + d) % 4, xh), z, s) for d in (1, 2, 3)]
    up, down = (p, (z + 1) % 8, s), (p, (z + 7) % 8, s)
    sibling, partner = (p + 1 - 2 * c, z, s), (p, z, 1 - s)
    for dev in (*y_peers, up, down, sibling, partner):
        signal(dev)
    keep_perm = pltpu.make_async_copy(perm_ref, perm_out.at[0], s_own)
    keep_perm.start()
    pl.semaphore_wait(barrier, 9 - own)

    def remote(src, dst, ssem, rsem, dev):
        return pltpu.make_async_remote_copy(
            src_ref=src, dst_ref=dst, send_sem=ssem, recv_sem=rsem, device_id=dev, device_id_type=MESH
        )

    sent = []

    def send(src, dst, ssem, rsem, dev):
        copy = remote(src, dst, ssem, rsem, dev)
        copy.start()
        sent.append(copy)

    def arrived(ref, rsem):
        remote(ref, ref, s_own, rsem, sibling).wait_recv()

    def lanes(z2, far=0):
        return pl.ds(pl.multiple_of(far * HALF + 128 * z2, 128), 128)

    src, dst = prot.at[:, lanes(z)], data.at[a, c, :, lanes(z, away)]
    send(src, dst, s1.at[1], r1.at[away], (device(a, 1 - xh), z, half))
    direct = remote(src, dst, s1.at[0], r1.at[away], (device(a, xh), z, half))

    @pl.when(own == 0)
    def _():
        direct.start()

    @pl.when(own == 1)
    def _():
        pltpu.make_async_copy(src, dst, r1.at[0]).start()

    send(perm_ref, perm_out.at[1], s_perm, rp, partner)

    def near(y2, z2):
        return data.at[y2, c, :, lanes(z2)]

    def near_all(z2):
        return data.at[:, c, :, lanes(z2)]

    def far(z2):
        return data.at[y, c, :, lanes(z2, 1)]

    def far_all(y2):
        return data.at[y2, c, :, pl.ds(HALF, HALF)]

    def ring(t, get, ssem, rsem):
        send(get((z + 8 - t) % 8), get((z + 8 - t) % 8), ssem.at[0, t], rsem.at[0, t], up)
        if t < 3:
            send(get((z + t) % 8), get((z + t) % 8), ssem.at[1, t], rsem.at[1, t], down)

    def ring_wait(t, get, rsem):
        arrived(get((z + 7 - t) % 8), rsem.at[0, t])
        if t < 3:
            arrived(get((z + 1 + t) % 8), rsem.at[1, t])

    arrived(near(y, z), r1.at[0])
    for d in (1, 2, 3):
        send(near(y, z), near(y, z), s2.at[d - 1], r2.at[d - 1], y_peers[d - 1])
    arrived(far(z), r1.at[1])
    ring(0, far, sb, rb)
    for d in (1, 2, 3):
        arrived(near((y + 4 - d) % 4, z), r2.at[d - 1])
    ring(0, near_all, sa, ra)
    for t in range(4):
        ring_wait(t, far, rb)
        if t < 3:
            ring(t + 1, far, sb, rb)

    def share(ref, k):
        send(ref, ref, sd.at[k], rd.at[k], sibling)

    for d in (1, 2, 3):
        send(far_all(y), far_all(y), s3.at[d - 1], r3.at[d - 1], y_peers[d - 1])
    share(near_all(z), 0)
    share(far_all(y), 8)
    for t in range(4):
        ring_wait(t, near_all, ra)
        if t < 3:
            ring(t + 1, near_all, sa, ra)
        share(near_all((z + 7 - t) % 8), 1 + t)
        if t < 3:
            share(near_all((z + 1 + t) % 8), 5 + t)
    for d in (1, 2, 3):
        arrived(far_all((y + 4 - d) % 4), r3.at[d - 1])
        share(far_all((y + 4 - d) % 4), 8 + d)

    def theirs_near(z2, k):
        arrived(data.at[:, 1 - c, :, lanes(z2)], rd.at[k])

    theirs_near(z, 0)
    for t in range(4):
        theirs_near((z + 7 - t) % 8, 1 + t)
        if t < 3:
            theirs_near((z + 1 + t) % 8, 5 + t)
    for d in range(4):
        arrived(data.at[(y + 4 - d) % 4, 1 - c, :, pl.ds(HALF, HALF)], rd.at[8 + d])
    arrived(perm_out.at[1], rp)
    keep_perm.wait()
    for copy in sent:
        copy.wait_send()

    @pl.when(own == 0)
    def _():
        direct.wait_send()


PROT_SPACE = pltpu.HBM


def gather_proteins(prot, perm_table):
    dma = pltpu.SemaphoreType.DMA
    space = pl.BlockSpec(memory_space=PROT_SPACE)
    return pl.pallas_call(
        protein_kernel,
        out_shape=[
            jax.ShapeDtypeStruct((4, 2, PB, ALL), jnp.bfloat16),
            jax.ShapeDtypeStruct((2, 4, HALF), jnp.int32),
        ],
        in_specs=[space, space],
        out_specs=[space, space],
        scratch_shapes=[
            dma, dma, dma, dma((2,)), dma((2,)), dma((3,)), dma((3,)), dma((2, 4)), dma((2, 4)),
            dma((2, 4)), dma((2, 4)), dma((3,)), dma((3,)), dma((12,)), dma((12,)),
        ],
        compiler_params=pltpu.CompilerParams(collective_id=1, has_side_effects=True, vmem_limit_bytes=16 * MIB),
        cost_estimate=pl.CostEstimate(flops=0, bytes_accessed=80 * MIB, transcendentals=0),
        name="gather_proteins",
    )(prot, perm_table)


def moments(a, b):
    a, b = a.astype(jnp.float32), b.astype(jnp.float32)
    mean = (jnp.sum(a, 1, keepdims=True) + jnp.sum(b, 1, keepdims=True)) / N
    var = (jnp.sum(a * a, 1, keepdims=True) + jnp.sum(b * b, 1, keepdims=True)) / N - mean * mean
    return mean, var


def scales(a, b):
    mean, var = moments(a, b)
    inv = jnp.sqrt(jnp.float32(N)) * lax.rsqrt(var + EPS)
    return inv / N, inv * mean


def as_rows(x, y):
    lane = lax.broadcasted_iota(jnp.int32, (x.shape[0], 128), 1)
    turned = jnp.transpose(jnp.where(lane == 0, x, y))
    return turned[0:1, :], turned[1:2, :]


MB = 256


def cis_kernel(plan, samp, perm, prot, g_ref, *refs):
    got = refs[:CIS_CHUNKS]
    out, stat, chosen, moved, sems = refs[CIS_CHUNKS:]
    k, m = pl.program_id(0), pl.program_id(1)

    @pl.when((k == 0) & (m == 0))
    def _():
        copies = []
        for i in range(8):
            row = pl.multiple_of(plan[PLAN_BLOCK + i] * VB, VB)
            copy = pltpu.make_async_copy(
                g_ref.at[pl.ds(row, VB)], chosen.at[pl.ds(i * VB, VB), pl.ds(0, HALF)], sems.at[i]
            )
            copy.start()
            copies.append(copy)
        for i in range(8):
            place = plan[PLAN_PLACE + i]
            for c in range(CIS_CHUNKS):

                @pl.when((place >= STARTS[c]) & (place < STARTS[c] + CHUNKS[c]))
                def _():
                    row = pl.multiple_of((place - STARTS[c]) * VB, VB)
                    chosen[i * VB : (i + 1) * VB, HALF:] = got[c][pl.ds(row, VB), :]

        for i in range(8):
            mean, var = moments(prot[i, :, :HALF], prot[i, :, HALF:])
            stat[0, i] = jnp.broadcast_to(mean, (PB, 128))
            stat[1, i] = jnp.broadcast_to(lax.rsqrt(var + EPS), (PB, 128))
        for copy in copies:
            copy.wait()

    here = lax.broadcasted_iota(jnp.int32, (MB, HALF), 0) + m * MB
    total = jnp.zeros((8 * VB, MB), jnp.float32)
    for side in range(2):
        goal = (perm[side, pl.ds(k, 1), :] + samp[0] * HALF) & (ALL - 1)
        hot = (goal == here).astype(jnp.float32).astype(jnp.bfloat16)
        total += dot_nt(chosen[:, side * HALF : (side + 1) * HALF], hot)
    total = total.astype(jnp.bfloat16)
    at = pl.ds(pl.multiple_of(m * MB, MB), MB)
    for i in range(8):
        moved[i, pl.ds(pl.multiple_of(k * VB, VB), VB), at] = total[i * VB : (i + 1) * VB]

    @pl.when((k == 3) & (m == ALL // MB - 1))
    def _():
        for i in range(8):
            rows = chosen[i * VB : (i + 1) * VB, :]
            by, off = scales(rows[:, :HALF], rows[:, HALF:])
            mean, inv = as_rows(stat[0, i], stat[1, i])
            cross = dot_nt(moved[i], prot[i])
            for j in range(4):
                u = cross[j * VB : (j + 1) * VB] * by - off * mean
                total = jnp.sum(u * u, 0, keepdims=True) * (inv * inv)
                out[i, j : j + 1, :PB] = jnp.where(plan[PLAN_KEEP + i] == 1, total, 0.0)


def cis(plan, samp, perm, prot, genotype, got):
    smem, vmem = pl.BlockSpec(memory_space=pltpu.SMEM), pl.BlockSpec(memory_space=pltpu.VMEM)
    return pl.pallas_call(
        cis_kernel,
        grid=(4, ALL // MB),
        out_shape=[
            jax.ShapeDtypeStruct((8, 4, 256), jnp.float32),
            jax.ShapeDtypeStruct((2, 8, PB, 128), jnp.float32),
        ],
        in_specs=[smem, smem, vmem, vmem, pl.BlockSpec(memory_space=pltpu.HBM), *[vmem] * CIS_CHUNKS],
        out_specs=[vmem, vmem],
        scratch_shapes=[
            pltpu.VMEM((8 * VB, ALL), jnp.bfloat16),
            pltpu.VMEM((8, 4 * VB, ALL), jnp.bfloat16),
            pltpu.SemaphoreType.DMA((8,)),
        ],
        compiler_params=pltpu.CompilerParams(vmem_limit_bytes=40 * MIB),
        cost_estimate=pl.CostEstimate(flops=20_000_000_000, bytes_accessed=20 * MIB, transcendentals=0),
        name="cis",
    )(plan, samp, perm, prot, genotype, *got[:CIS_CHUNKS])


def cis_sum_kernel(part, out, near, every, mine, s1, r1, s2, r2):
    p, z, s = lax.axis_index("prot"), lax.axis_index("var"), lax.axis_index("samp")
    home = 8 * s + z
    same = lax.rem(p + 16 - home, 16)
    is_home = 1 - (same + 15) // 16
    barrier = pltpu.get_barrier_semaphore()

    def signal(dev):
        pl.semaphore_signal(barrier, inc=1, device_id=dev, device_id_type=MESH)

    for d in range(1, 8):
        signal((p, (z + d) % 8, s))
    for d in range(16):
        dev = ((p + d) % 16, p % 8, p // 8)
        if d == 0:

            @pl.when(is_home == 0)
            def _():
                signal(dev)
        else:
            signal(dev)
    pl.semaphore_wait(barrier, 23 - is_home)

    def copy_to(src, dst, ssem, rsem, dev):
        return pltpu.make_async_remote_copy(
            src_ref=src, dst_ref=dst, send_sem=ssem, recv_sem=rsem, device_id=dev, device_id_type=MESH
        )

    sent = []
    for d in range(1, 8):
        z2 = (z + d) % 8
        copy = copy_to(part.at[z2], near.at[d], s1.at[d], r1.at[d], (p, z2, s))
        copy.start()
        sent.append(copy)
    total = part[z]
    for d, copy in enumerate(sent, 1):
        copy.wait_recv()
        total += near[d]
    mine[...] = total
    last = []
    for dz in range(8):
        for ds in range(2):
            dev = (home, (z + dz) % 8, (s + ds) % 2)
            copy = copy_to(mine, every.at[p], s2.at[dz * 2 + ds], r2.at[p], dev)
            if dz == ds == 0:

                @pl.when(is_home == 0)
                def _():
                    copy.start()

                @pl.when(is_home == 1)
                def _():
                    pltpu.make_async_copy(mine, every.at[p], r2.at[p]).start()

                last.append(copy)
            else:
                copy.start()
                sent.append(copy)
    total = jnp.zeros_like(mine)
    for d in range(16):
        copy_to(mine, every.at[d], s2.at[0], r2.at[d], (p, (z + 1) % 8, s)).wait_recv()
        total += every[d]
    out[...] = total
    for copy in sent:
        copy.wait_send()

    @pl.when(is_home == 0)
    def _():
        last[0].wait_send()


def cis_sum(part):
    dma = pltpu.SemaphoreType.DMA
    return pl.pallas_call(
        cis_sum_kernel,
        out_shape=jax.ShapeDtypeStruct((4, 256), jnp.float32),
        in_specs=[pl.BlockSpec(memory_space=pltpu.VMEM)],
        out_specs=pl.BlockSpec(memory_space=pltpu.VMEM),
        scratch_shapes=[
            pltpu.VMEM((8, 4, 256), jnp.float32),
            pltpu.VMEM((16, 4, 256), jnp.float32),
            pltpu.VMEM((4, 256), jnp.float32),
            dma((8,)), dma((8,)), dma((16,)), dma((16,)),
        ],
        compiler_params=pltpu.CompilerParams(collective_id=2, has_side_effects=True),
        cost_estimate=pl.CostEstimate(flops=0, bytes_accessed=16 * MIB, transcendentals=0),
        name="cis_sum",
    )(part)


def trans_kernel(chunks, first, last, aliased, plan, prot, stat, g_ref, *refs):
    got = refs[:chunks]
    out, near, far, stage, s_near, s_far, s_out = refs[chunks + aliased :]
    steps = [(t, min(t + 2, last)) for t in range(first, last, 2)]

    def fetch(n):
        lo, hi = steps[n]
        slot = n % 2
        for t in range(lo, hi):
            tile = plan[PLAN_TILE + t]
            at = (t - lo) * 128
            row = pl.multiple_of(tile * 128, 128)
            pltpu.make_async_copy(
                g_ref.at[pl.ds(row, 128)], near.at[slot, pl.ds(at, 128)], s_near.at[slot, t - lo]
            ).start()
            for h in range(2):
                place = plan[tile * 2 + h]
                for c in range(chunks):

                    @pl.when((place >= STARTS[c]) & (place < STARTS[c] + CHUNKS[c]))
                    def _():
                        row = pl.multiple_of((place - STARTS[c]) * VB, VB)
                        pltpu.make_async_copy(
                            got[c].at[pl.ds(row, VB)],
                            far.at[slot, pl.ds(at + h * VB, VB)],
                            s_far.at[slot, (t - lo) * 2 + h],
                        ).start()

    def fetched(n):
        lo, hi = steps[n]
        slot = n % 2
        for t in range(lo, hi):
            at = (t - lo) * 128
            pltpu.make_async_copy(
                g_ref.at[pl.ds(0, 128)], near.at[slot, pl.ds(at, 128)], s_near.at[slot, t - lo]
            ).wait()
            for h in range(2):
                pltpu.make_async_copy(
                    got[0].at[pl.ds(0, VB)],
                    far.at[slot, pl.ds(at + h * VB, VB)],
                    s_far.at[slot, (t - lo) * 2 + h],
                ).wait()

    def written(n):
        lo, hi = steps[n]
        slot = n % 2
        for t in range(lo, hi):
            pltpu.make_async_copy(
                stage.at[slot, :, pl.ds((t - lo) * 128, 128)], out.at[:, pl.ds(0, 128)], s_out.at[slot, t - lo]
            ).wait()

    fetch(0)
    for n, (lo, hi) in enumerate(steps):
        slot, width = n % 2, (hi - lo) * 128
        if n + 1 < len(steps):
            fetch(n + 1)
        fetched(n)
        a, b = near[slot, :width, :], far[slot, :width, :]
        by, off = as_rows(*scales(a, b))
        if n >= 2:
            written(n - 2)
        for i in range(8):
            at = slice(i * PB, (i + 1) * PB)
            cross = dot_nt(prot[at, :HALF], a) + dot_nt(prot[at, HALF:], b)
            mean, inv = stat[0, i][:, :1], stat[1, i][:, :1]
            stage[slot, at, :width] = ((cross * by - mean * off) * inv).astype(jnp.bfloat16)
        for t in range(lo, hi):
            column = pl.multiple_of(plan[PLAN_TILE + t] * 128, 128)
            pltpu.make_async_copy(
                stage.at[slot, :, pl.ds((t - lo) * 128, 128)], out.at[:, pl.ds(column, 128)], s_out.at[slot, t - lo]
            ).start()
    for n in range(max(len(steps) - 2, 0), len(steps)):
        written(n)


def trans(chunks, first, last, plan, prot, stat, genotype, got, out):
    vmem, hbm = pl.BlockSpec(memory_space=pltpu.VMEM), pl.BlockSpec(memory_space=pltpu.HBM)
    operands = [plan, prot, stat, genotype, *got[:chunks]]
    specs = [pl.BlockSpec(memory_space=pltpu.SMEM), vmem, vmem, *[hbm] * (1 + chunks)]
    aliases = {}
    if out is not None:
        aliases = {len(operands): 0}
        operands.append(out)
        specs.append(hbm)
    wide = min(2, last - first) * 128
    dma = pltpu.SemaphoreType.DMA
    return pl.pallas_call(
        functools.partial(trans_kernel, chunks, first, last, len(aliases)),
        out_shape=jax.ShapeDtypeStruct((COLS, ROWS), jnp.bfloat16),
        in_specs=specs,
        out_specs=hbm,
        scratch_shapes=[
            pltpu.VMEM((2, wide, HALF), jnp.bfloat16),
            pltpu.VMEM((2, wide, HALF), jnp.bfloat16),
            pltpu.VMEM((2, COLS, wide), jnp.bfloat16),
            dma((2, 2)), dma((2, 4)), dma((2, 2)),
        ],
        input_output_aliases=aliases,
        compiler_params=pltpu.CompilerParams(vmem_limit_bytes=24 * MIB),
        cost_estimate=pl.CostEstimate(
            flops=2 * COLS * ALL * 128 * (last - first), bytes_accessed=8 * MIB, transcendentals=0
        ),
        name="trans",
    )(*operands)


def body(genotype, proteins, cis_pick, perm_table):
    samp = lax.axis_index("samp").astype(jnp.int32).reshape(1)
    mine = sort_blocks(cis_pick, genotype)
    got = [lax.ppermute(chunk, "samp", [(0, 1), (1, 0)]) for chunk in mine]
    plan = make_plan(cis_pick)
    data, perm = gather_proteins(proteins.T, perm_table)
    prot = data.reshape(8, PB, ALL)
    part, stat = cis(plan, samp, perm, prot, genotype, got)
    cis_stat = cis_sum(part)[:, :PB] / jnp.float32(8 * HALF)
    out = None
    for chunks, first, last in GROUPS:
        out = trans(chunks, first, last, plan, prot.reshape(COLS, ALL), stat, genotype, got, out)
    return out.T, cis_stat


def solution(mesh):
    return jax.shard_map(
        body,
        mesh=mesh,
        in_specs=(
            P(("prot", "var"), "samp"),
            P("samp", "prot"),
            P(("prot", "var"), None),
            P(None, "samp"),
        ),
        out_specs=(P(("prot", "var"), "samp"), P(None, "prot")),
        check_vma=False,
    )
```

```python
import functools

import jax
import jax.numpy as jnp
from jax import lax
from jax.experimental import pallas as pl
from jax.experimental.pallas import tpu as pltpu
from jax.sharding import PartitionSpec as P

MESH = pl.DeviceIdType.MESH
VB = 64
BLOCKS = 24
TILES = BLOCKS // 2
ROWS = VB * BLOCKS
HALF = 1024
ALL = 2 * HALF
PB = 184
COLS = 8 * PB
CHUNKS = (8, 8, 4, 4)
STARTS = tuple(sum(CHUNKS[:c]) for c in range(len(CHUNKS)))
GROUPS = ((2, 0, 8), (3, 8, 10), (4, 10, 12))
EPS = 1e-6
N = float(ALL)
MIB = 1 << 20
NT = (((1,), (1,)), ((), ()))


def dot_nt(a, b):
    return lax.dot_general(a, b, NT, preferred_element_type=jnp.float32)


PLAN_TILE, PLAN_PLACE, PLAN_KEEP, PLAN = 24, 36, 44, 64


def block_order(pick_ref, first, flag, order):
    for b in range(BLOCKS):
        flag[b] = jnp.int32(0)
    for i in range(8):
        flag[pick_ref[0, first + i] & 31] = jnp.int32(1)
    flags = [flag[b] for b in range(BLOCKS)]
    at = jnp.int32(0)
    for rank in range(3):
        for b in range(BLOCKS):
            mine, pair = flags[b], flags[b ^ 1]
            order[at] = jnp.int32(b)
            at = at + (mine, (1 - mine) & pair, (1 - mine) & (1 - pair))[rank]


def sort_kernel(pick_ref, g_ref, *refs):
    outs, (chosen, plan, flag, order, seen) = refs[: len(CHUNKS)], refs[len(CHUNKS) :]
    samp = lax.axis_index("samp")
    block_order(pick_ref, 8 * (1 - samp), flag, order)
    for c, blocks in enumerate(CHUNKS):
        for t in range(blocks):
            row = pl.multiple_of(order[STARTS[c] + t] * VB, VB)
            outs[c][t * VB : (t + 1) * VB, :] = g_ref[pl.ds(row, VB), :]

    block_order(pick_ref, 8 * samp, flag, order)
    for t in range(TILES):
        seen[t] = jnp.int32(0)
    done = jnp.int32(0)
    for r in range(BLOCKS):
        b = order[r]
        plan[b] = jnp.int32(r)
        t = lax.shift_right_logical(b, 1)
        before = seen[t]
        seen[t] = before + 1
        plan[PLAN_TILE + done] = t
        done = done + before
    for i in range(8):
        pick = pick_ref[0, 8 * samp + i]
        keep = (pick >= 0).astype(jnp.int32)
        block = jnp.maximum(pick, 0)
        plan[PLAN_PLACE + i] = plan[block] * keep
        plan[PLAN_KEEP + i] = keep
        chosen[i * VB : (i + 1) * VB, :] = g_ref[pl.ds(pl.multiple_of(block * VB, VB), VB), :]


def sort_blocks(pick, genotype):
    smem, vmem = pl.BlockSpec(memory_space=pltpu.SMEM), pl.BlockSpec(memory_space=pltpu.VMEM)
    *mine, chosen, plan = pl.pallas_call(
        sort_kernel,
        out_shape=[
            *[jax.ShapeDtypeStruct((b * VB, HALF), jnp.bfloat16) for b in CHUNKS],
            jax.ShapeDtypeStruct((8 * VB, HALF), jnp.bfloat16),
            jax.ShapeDtypeStruct((PLAN,), jnp.int32),
        ],
        in_specs=[smem, vmem],
        out_specs=[vmem] * (len(CHUNKS) + 1) + [smem],
        scratch_shapes=[pltpu.SMEM((n,), jnp.int32) for n in (32, 32, TILES)],
        compiler_params=pltpu.CompilerParams(vmem_limit_bytes=14 * MIB),
        name="sort_blocks",
    )(pick, genotype)
    return mine, chosen, plan


def choose_kernel(plan, got, chosen):
    for i in range(8):
        row = pl.multiple_of(plan[PLAN_PLACE + i] * VB, VB)
        chosen[i * VB : (i + 1) * VB, :] = got[pl.ds(row, VB), :]


def choose(plan, got):
    vmem = pl.BlockSpec(memory_space=pltpu.VMEM)
    return pl.pallas_call(
        choose_kernel,
        out_shape=jax.ShapeDtypeStruct((8 * VB, HALF), jnp.bfloat16),
        in_specs=[pl.BlockSpec(memory_space=pltpu.SMEM), vmem],
        out_specs=vmem,
        compiler_params=pltpu.CompilerParams(vmem_limit_bytes=4 * MIB),
        name="choose",
    )(plan, got)


MB = 256


def move_step(m, goals, chosen, store):
    here = lax.broadcasted_iota(jnp.int32, (MB, HALF), 0) + m * MB
    at = pl.ds(pl.multiple_of(m * MB, MB), MB)
    for k in range(4):
        hot = jnp.where(goals[k : k + 1, :] == here, 1.0, 0.0).astype(jnp.bfloat16)
        total = dot_nt(chosen[...], hot).astype(jnp.bfloat16)
        for i in range(8):
            store((i, slice(k * VB, (k + 1) * VB), at), total[i * VB : (i + 1) * VB])


def protein_kernel(prot, perm, chosen, data, moved, goals, s_own, s1, r1, s2, r2, sa, ra, sb, rb, s3, r3, sd, rd):
    p, z, s = lax.axis_index("prot"), lax.axis_index("var"), lax.axis_index("samp")
    c, xh, y = p % 2, (p // 2) % 2, p // 4
    half, a = y // 2, (y % 2) * 2 + xh
    away = (s + half) % 2

    def device(y2, x2):
        return y2 * 4 + x2 * 2 + c

    barrier = pltpu.get_barrier_semaphore()

    def signal(dev):
        pl.semaphore_signal(barrier, inc=1, device_id=dev, device_id_type=MESH)

    source = device(2 * s + y // 2, y % 2)
    y_peers = [(device((y + d) % 4, xh), z, s) for d in (1, 2, 3)]
    up, down = (p, (z + 1) % 8, s), (p, (z + 7) % 8, s)
    sibling = (p + 1 - 2 * c, z, s)
    for dev in ((source, (z + 7) % 8, s), (source, (z + 7) % 8, 1 - s), *y_peers, up, down, sibling):
        signal(dev)
    goals[...] = (perm[...] + s * HALF) & (ALL - 1)
    pl.semaphore_wait(barrier, 8)

    def remote(src, dst, ssem, rsem, dev):
        return pltpu.make_async_remote_copy(
            src_ref=src, dst_ref=dst, send_sem=ssem, recv_sem=rsem, device_id=dev, device_id_type=MESH
        )

    def send(src, dst, ssem, rsem, dev):
        remote(src, dst, ssem, rsem, dev).start()

    def arrived(ref, rsem):
        remote(ref, ref, s_own, rsem, sibling).wait_recv()

    def left(ref, ssem):
        remote(ref, ref, ssem, s_own, sibling).wait_send()

    def lanes(z2, far=0):
        return pl.ds(pl.multiple_of(far * HALF + 128 * z2, 128), 128)

    def near(y2, z2):
        return data.at[y2, c, :, lanes(z2)]

    def near_all(z2):
        return data.at[:, c, :, lanes(z2)]

    def far(y2, z2):
        return data.at[y2, c, :, lanes(z2, 1)]

    def far_all(y2):
        return data.at[y2, c, :, pl.ds(HALF, HALF)]

    def pass_near(t, k, downward=True):
        y2 = (y + 4 - k) % 4
        here = near(y2, (z + 8 - t) % 8)
        send(here, here, sa.at[0, t, k], ra.at[0, t, k], up)

        @pl.when(t < 3)
        def _():
            here = near(y2, (z + t) % 8)
            send(here, here, sa.at[1, t, k], ra.at[1, t, k], down)

    def pass_far(t):
        here = far(y, (z + 8 - t) % 8)
        send(here, here, sb.at[0, t], rb.at[0, t], up)

        @pl.when(t < 3)
        def _():
            here = far(y, (z + t) % 8)
            send(here, here, sb.at[1, t], rb.at[1, t], down)

    def spread_far(dz):
        here = far(y, (z + dz) % 8)
        for d in (1, 2, 3):
            send(here, here, s3.at[d - 1, dz], r3.at[d - 1, dz], y_peers[d - 1])

    def share(ref, k):
        send(ref, ref, sd.at[k], rd.at[k], sibling)

    def ring(t):
        arrived(far(y, (z + 7 - t) % 8), rb.at[0, t])

        @pl.when(t < 3)
        def _():
            arrived(far(y, (z + 1 + t) % 8), rb.at[1, t])
            pass_far(t + 1)
            spread_far(1 + t)

        spread_far(7 - t)
        for k in range(4):
            y2 = (y + 4 - k) % 4
            arrived(near(y2, (z + 7 - t) % 8), ra.at[0, t, k])

            @pl.when(t < 3)
            def _():
                arrived(near(y2, (z + 1 + t) % 8), ra.at[1, t, k])
                pass_near(t + 1, k)

        share(near_all((z + 7 - t) % 8), 1 + t)

        @pl.when(t < 3)
        def _():
            share(near_all((z + 1 + t) % 8), 5 + t)

    def step(n, _):
        @pl.when(n == 0)
        def _():
            z2 = (z + 1) % 8
            src, dst = prot.at[:, lanes(z2)], data.at[a, c, :, lanes(z2, away)]
            for x2 in range(2):
                send(src, dst, s1.at[x2], r1.at[away], (device(a, x2), z2, half))

        @pl.when(n == 1)
        def _():
            arrived(near(y, z), r1.at[0])
            for d in (1, 2, 3):
                send(near(y, z), near(y, z), s2.at[d - 1], r2.at[d - 1], y_peers[d - 1])
            pass_near(0, 0)
            arrived(far(y, z), r1.at[1])
            pass_far(0)
            spread_far(0)

        @pl.when(n == 2)
        def _():
            for d in (1, 2, 3):
                arrived(near((y + 4 - d) % 4, z), r2.at[d - 1])
                pass_near(0, d)
            share(near_all(z), 0)

        @pl.when((n >= 2) & (n < 6))
        def _():
            ring(n - 2)

        move_step(n, goals, chosen, lambda at, value: moved.__setitem__(at, value))
        return 0

    lax.fori_loop(0, ALL // MB, step, 0)
    share(far_all(y), 8)
    for d in (1, 2, 3):
        for dz in range(8):
            arrived(far((y + 4 - d) % 4, (z + dz) % 8), r3.at[d - 1, dz])
        share(far_all((y + 4 - d) % 4), 8 + d)

    def theirs_near(z2, k):
        arrived(data.at[:, 1 - c, :, lanes(z2)], rd.at[k])

    theirs_near(z, 0)
    for t in range(4):
        theirs_near((z + 7 - t) % 8, 1 + t)
        if t < 3:
            theirs_near((z + 1 + t) % 8, 5 + t)
    for d in range(4):
        arrived(data.at[(y + 4 - d) % 4, 1 - c, :, pl.ds(HALF, HALF)], rd.at[8 + d])

    one = near(y, z)
    for x2 in range(2):
        left(one, s1.at[x2])
    for d in range(3):
        left(one, s2.at[d])
        for dz in range(8):
            left(one, s3.at[d, dz])
    for t in range(4):
        for way in range(2 if t < 3 else 1):
            left(one, sb.at[way, t])
            for k in range(4):
                left(one, sa.at[way, t, k])
    for k in range(8):
        left(near_all(z), sd.at[k])
    for k in range(8, 12):
        left(far_all(y), sd.at[k])


def gather_proteins(prot, perm, chosen):
    dma = pltpu.SemaphoreType.DMA
    space, vmem = pl.BlockSpec(memory_space=pl.ANY), pl.BlockSpec(memory_space=pltpu.VMEM)
    return pl.pallas_call(
        protein_kernel,
        out_shape=[
            jax.ShapeDtypeStruct((4, 2, PB, ALL), jnp.bfloat16),
            jax.ShapeDtypeStruct((8, 4 * VB, ALL), jnp.bfloat16),
        ],
        in_specs=[space, vmem, vmem],
        out_specs=[space, vmem],
        scratch_shapes=[
            pltpu.VMEM((4, HALF), jnp.int32),
            dma, dma((2,)), dma((2,)), dma((3,)), dma((3,)), dma((2, 4, 4)), dma((2, 4, 4)),
            dma((2, 4)), dma((2, 4)), dma((3, 8)), dma((3, 8)), dma((12,)), dma((12,)),
        ],
        compiler_params=pltpu.CompilerParams(collective_id=1, has_side_effects=True, vmem_limit_bytes=24 * MIB),
        cost_estimate=pl.CostEstimate(flops=9_000_000_000, bytes_accessed=80 * MIB, transcendentals=0),
        name="gather_proteins",
    )(prot, perm, chosen)


def moments(a, b):
    a, b = a.astype(jnp.float32), b.astype(jnp.float32)
    mean = (jnp.sum(a, 1, keepdims=True) + jnp.sum(b, 1, keepdims=True)) / N
    var = (jnp.sum(a * a, 1, keepdims=True) + jnp.sum(b * b, 1, keepdims=True)) / N - mean * mean
    return mean, var


def scales(a, b):
    mean, var = moments(a, b)
    inv = jnp.sqrt(jnp.float32(N)) * lax.rsqrt(var + EPS)
    return inv / N, inv * mean


def as_rows(x, y):
    lane = lax.broadcasted_iota(jnp.int32, (x.shape[0], 128), 1)
    turned = jnp.transpose(jnp.where(lane == 0, x, y))
    return turned[0:1, :], turned[1:2, :]


def cis_kernel(plan, perm, prot, chosen_own, chosen, moved_own, out, stat, goals, moved, part, sums, near, every, s1, r1, s2, r2):
    p, z, s = lax.axis_index("prot"), lax.axis_index("var"), lax.axis_index("samp")
    barrier = pltpu.get_barrier_semaphore()

    def signal(dev):
        pl.semaphore_signal(barrier, inc=1, device_id=dev, device_id_type=MESH)

    for d in range(1, 8):
        signal((p, (z + d) % 8, s))
    home = p % 8
    at_home = 1 - ((z - home) * (z - home) + 63) // 64
    for d in range(16):
        signal((d, (home + at_home) % 8, p // 8))

    goals[...] = (perm[...] + s * HALF) & (ALL - 1)

    def store(at, value):
        moved[at] = moved_own[at] + value

    def move(m, _):
        move_step(m, goals, chosen, store)
        return 0

    lax.fori_loop(0, ALL // MB, move, 0)
    pl.semaphore_wait(barrier, 23)

    def remote(src, dst, ssem, rsem, dev):
        return pltpu.make_async_remote_copy(
            src_ref=src, dst_ref=dst, send_sem=ssem, recv_sem=rsem, device_id=dev, device_id_type=MESH
        )

    def block(n, _):
        i = (z + 1 + n) % 8
        mean, var = moments(prot[i, :, :HALF], prot[i, :, HALF:])
        inv = lax.rsqrt(var + EPS)
        stat[0, i] = jnp.broadcast_to(mean, (PB, 128))
        stat[1, i] = jnp.broadcast_to(inv, (PB, 128))
        mean, inv = as_rows(mean, inv)
        rows = pl.ds(pl.multiple_of(i * VB, VB), VB)
        by, off = scales(chosen_own[rows, :], chosen[rows, :])
        cross = dot_nt(moved[i], prot[i])
        keep = plan[PLAN_KEEP + i].astype(jnp.float32)
        for k in range(4):
            u = cross[k * VB : (k + 1) * VB] * by - off * mean
            part[i, k : k + 1, :PB] = jnp.sum(u * u, 0, keepdims=True) * (inv * inv) * keep

        @pl.when(n != 7)
        def _():
            remote(part.at[i], near.at[0, n], s1.at[0, n], r1.at[0, n], (p, i, s)).start()

        @pl.when(n != 6)
        def _():
            remote(part.at[i], near.at[1, n], s1.at[1, n], r1.at[1, n], (p, (i + 1) % 8, s)).start()

        return 0

    part[...] = jnp.zeros_like(part)
    lax.fori_loop(0, 8, block, 0)

    own_sends = []
    for side in range(2):
        total = part[(z + 8 - side) % 8]
        for n in range(8):
            if n != 7 - side:
                remote(part.at[0], near.at[side, n], s1.at[side, n], r1.at[side, n], (p, (z + 1) % 8, s)).wait_recv()
                total += near[side, n]
        sums[side] = total
        for ds in range(2):
            for dz in range(1, 8) if side == 0 else (7,):
                to = (8 * s + (z + 8 - side) % 8, (z + dz) % 8, (s + ds) % 2)
                copy = remote(sums.at[side], every.at[p], s2.at[side, ds, dz], r2.at[p], to)
                copy.start()
                own_sends.append(copy)
    total = jnp.zeros((4, 256), jnp.float32)
    for d in range(16):
        remote(sums.at[0], every.at[d], s2.at[0, 0, 0], r2.at[d], (p, (z + 1) % 8, s)).wait_recv()
        total += every[d]
    out[...] = total
    for copy in own_sends:
        copy.wait_send()
    for side in range(2):
        for n in range(8):
            if n != 7 - side:
                remote(part.at[0], near.at[side, n], s1.at[side, n], r1.at[side, n], (p, (z + 1) % 8, s)).wait_send()


def cis(plan, perm, prot, chosen_own, chosen_got, moved):
    smem, vmem = pl.BlockSpec(memory_space=pltpu.SMEM), pl.BlockSpec(memory_space=pltpu.VMEM)
    dma = pltpu.SemaphoreType.DMA
    return pl.pallas_call(
        cis_kernel,
        out_shape=[
            jax.ShapeDtypeStruct((4, 256), jnp.float32),
            jax.ShapeDtypeStruct((2, 8, PB, 128), jnp.float32),
        ],
        in_specs=[smem, *[vmem] * 5],
        out_specs=[vmem, vmem],
        scratch_shapes=[
            pltpu.VMEM((4, HALF), jnp.int32),
            pltpu.VMEM((8, 4 * VB, ALL), jnp.bfloat16),
            pltpu.VMEM((8, 4, 256), jnp.float32),
            pltpu.VMEM((2, 4, 256), jnp.float32),
            pltpu.VMEM((2, 8, 4, 256), jnp.float32),
            pltpu.VMEM((16, 4, 256), jnp.float32),
            dma((2, 8)), dma((2, 8)), dma((2, 2, 8)), dma((16,)),
        ],
        compiler_params=pltpu.CompilerParams(collective_id=2, has_side_effects=True, vmem_limit_bytes=36 * MIB),
        cost_estimate=pl.CostEstimate(flops=12_000_000_000, bytes_accessed=20 * MIB, transcendentals=0),
        name="cis",
    )(plan, perm, prot, chosen_own, chosen_got, moved)


def trans_kernel(chunks, first, last, aliased, plan, prot, stat, g_ref, *refs):
    got = refs[:chunks]
    out, rows, stage, sems = refs[chunks + aliased :]
    steps = (last - first) // 2

    def copy_out(n, h):
        column = pl.multiple_of(plan[PLAN_TILE + first + 2 * n + h] * 128, 128)
        return pltpu.make_async_copy(
            stage.at[n % 2, :, pl.ds(h * 128, 128)], out.at[:, pl.ds(column, 128)], sems.at[n % 2, h]
        )

    def step(n, _):
        for t in range(2):
            tile = plan[PLAN_TILE + first + 2 * n + t]
            at = t * 128
            rows[at : at + 128, :HALF] = g_ref[pl.ds(pl.multiple_of(tile * 128, 128), 128), :]
            for h in range(2):
                place = plan[tile * 2 + h]
                for c in range(chunks):

                    @pl.when((place >= STARTS[c]) & (place < STARTS[c] + CHUNKS[c]))
                    def _():
                        row = pl.multiple_of((place - STARTS[c]) * VB, VB)
                        rows[at + h * VB : at + (h + 1) * VB, HALF:] = got[c][pl.ds(row, VB), :]

        both = rows[...]
        by, off = as_rows(*scales(both[:, :HALF], both[:, HALF:]))
        cross = dot_nt(prot[...], both)
        mean = jnp.concatenate([stat[0], stat[0]], 1)
        inv = jnp.concatenate([stat[1], stat[1]], 1)

        @pl.when(n >= 2)
        def _():
            for h in range(2):
                copy_out(n - 2, h).wait()

        stage[n % 2] = ((cross * by - mean * off) * inv).astype(jnp.bfloat16)
        for h in range(2):
            copy_out(n, h).start()
        return 0

    lax.fori_loop(0, steps, step, 0)
    for n in range(max(steps - 2, 0), steps):
        for h in range(2):
            copy_out(n, h).wait()


def trans(chunks, first, last, plan, prot, stat, genotype, got, out):
    vmem, hbm = pl.BlockSpec(memory_space=pltpu.VMEM), pl.BlockSpec(memory_space=pltpu.HBM)
    operands = [plan, prot, stat, genotype, *got[:chunks]]
    specs = [pl.BlockSpec(memory_space=pltpu.SMEM), *[vmem] * (3 + chunks)]
    aliases = {}
    if out is not None:
        aliases = {len(operands): 0}
        operands.append(out)
        specs.append(hbm)
    return pl.pallas_call(
        functools.partial(trans_kernel, chunks, first, last, len(aliases)),
        out_shape=jax.ShapeDtypeStruct((COLS, ROWS), jnp.bfloat16),
        in_specs=specs,
        out_specs=hbm,
        scratch_shapes=[
            pltpu.VMEM((256, ALL), jnp.bfloat16),
            pltpu.VMEM((2, COLS, 256), jnp.bfloat16),
            pltpu.SemaphoreType.DMA((2, 2)),
        ],
        input_output_aliases=aliases,
        compiler_params=pltpu.CompilerParams(vmem_limit_bytes=24 * MIB),
        cost_estimate=pl.CostEstimate(
            flops=2 * COLS * ALL * 128 * (last - first), bytes_accessed=8 * MIB, transcendentals=0
        ),
        name="trans",
    )(*operands)


SWAP = [(0, 1), (1, 0)]


def body(genotype, proteins, cis_pick, perm_table):
    perm_got = lax.ppermute(perm_table, "samp", SWAP)
    mine, chosen, plan = sort_blocks(cis_pick, genotype)
    got = [lax.ppermute(chunk, "samp", SWAP) for chunk in mine]
    data, moved = gather_proteins(proteins.T, perm_table, chosen)
    prot = data.reshape(8, PB, ALL)
    total, stat = cis(plan, perm_got, prot, chosen, choose(plan, got[0]), moved)
    cis_stat = total[:, :PB] / jnp.float32(8 * HALF)
    out = None
    for chunks, first, last in GROUPS:
        out = trans(chunks, first, last, plan, prot.reshape(COLS, ALL), stat.reshape(2, COLS, 128), genotype, got, out)
    return out.T, cis_stat


def solution(mesh):
    return jax.shard_map(
        body,
        mesh=mesh,
        in_specs=(
            P(("prot", "var"), "samp"),
            P("samp", "prot"),
            P(("prot", "var"), None),
            P(None, "samp"),
        ),
        out_specs=(P(("prot", "var"), "samp"), P(None, "prot")),
        check_vma=False,
    )
```

```python
import functools

import jax
import jax.numpy as jnp
from jax import lax
from jax.experimental import pallas as pl
from jax.experimental.pallas import tpu as pltpu
from jax.sharding import PartitionSpec as P

MESH = pl.DeviceIdType.MESH
VB = 64
BLOCKS = 24
TILES = BLOCKS // 2
ROWS = VB * BLOCKS
HALF = 1024
ALL = 2 * HALF
PB = 184
COLS = 8 * PB
CHUNKS = (8, 16)
STARTS = tuple(sum(CHUNKS[:c]) for c in range(len(CHUNKS)))
GROUPS = ((2, 0, 12),)
EPS = 1e-6
N = float(ALL)
MIB = 1 << 20
NT = (((1,), (1,)), ((), ()))


def dot_nt(a, b):
    return lax.dot_general(a, b, NT, preferred_element_type=jnp.float32)


PLAN_TILE, PLAN_PLACE, PLAN_KEEP, PLAN = 24, 36, 44, 64


def block_order(pick_ref, first, flag, order):
    for b in range(BLOCKS):
        flag[b] = jnp.int32(0)
    for i in range(8):
        flag[pick_ref[0, first + i] & 31] = jnp.int32(1)
    flags = [flag[b] for b in range(BLOCKS)]
    at = jnp.int32(0)
    for rank in range(3):
        for b in range(BLOCKS):
            mine, pair = flags[b], flags[b ^ 1]
            order[at] = jnp.int32(b)
            at = at + (mine, (1 - mine) & pair, (1 - mine) & (1 - pair))[rank]


def sort_kernel(pick_ref, g_ref, *refs):
    outs, (chosen, plan, flag, order, seen) = refs[: len(CHUNKS)], refs[len(CHUNKS) :]
    samp = lax.axis_index("samp")
    block_order(pick_ref, 8 * (1 - samp), flag, order)
    for c, blocks in enumerate(CHUNKS):
        for t in range(blocks):
            row = pl.multiple_of(order[STARTS[c] + t] * VB, VB)
            outs[c][t * VB : (t + 1) * VB, :] = g_ref[pl.ds(row, VB), :]

    block_order(pick_ref, 8 * samp, flag, order)
    for t in range(TILES):
        seen[t] = jnp.int32(0)
    done = jnp.int32(0)
    for r in range(BLOCKS):
        b = order[r]
        plan[b] = jnp.int32(r)
        t = lax.shift_right_logical(b, 1)
        before = seen[t]
        seen[t] = before + 1
        plan[PLAN_TILE + done] = t
        done = done + before
    for i in range(8):
        pick = pick_ref[0, 8 * samp + i]
        keep = (pick >= 0).astype(jnp.int32)
        block = jnp.maximum(pick, 0)
        plan[PLAN_PLACE + i] = plan[block] * keep
        plan[PLAN_KEEP + i] = keep
        chosen[i * VB : (i + 1) * VB, :] = g_ref[pl.ds(pl.multiple_of(block * VB, VB), VB), :]


def sort_blocks(pick, genotype):
    smem, vmem = pl.BlockSpec(memory_space=pltpu.SMEM), pl.BlockSpec(memory_space=pltpu.VMEM)
    *mine, chosen, plan = pl.pallas_call(
        sort_kernel,
        out_shape=[
            *[jax.ShapeDtypeStruct((b * VB, HALF), jnp.bfloat16) for b in CHUNKS],
            jax.ShapeDtypeStruct((8 * VB, HALF), jnp.bfloat16),
            jax.ShapeDtypeStruct((PLAN,), jnp.int32),
        ],
        in_specs=[smem, vmem],
        out_specs=[vmem] * (len(CHUNKS) + 1) + [smem],
        scratch_shapes=[pltpu.SMEM((n,), jnp.int32) for n in (32, 32, TILES)],
        compiler_params=pltpu.CompilerParams(vmem_limit_bytes=14 * MIB),
        name="sort_blocks",
    )(pick, genotype)
    return mine, chosen, plan


def choose_kernel(plan, got, chosen):
    for i in range(8):
        row = pl.multiple_of(plan[PLAN_PLACE + i] * VB, VB)
        chosen[i * VB : (i + 1) * VB, :] = got[pl.ds(row, VB), :]


def choose(plan, got):
    vmem = pl.BlockSpec(memory_space=pltpu.VMEM)
    return pl.pallas_call(
        choose_kernel,
        out_shape=jax.ShapeDtypeStruct((8 * VB, HALF), jnp.bfloat16),
        in_specs=[pl.BlockSpec(memory_space=pltpu.SMEM), vmem],
        out_specs=vmem,
        compiler_params=pltpu.CompilerParams(vmem_limit_bytes=4 * MIB),
        name="choose",
    )(plan, got)


MB = 256


def move_step(m, goals, chosen, store):
    here = lax.broadcasted_iota(jnp.int32, (MB, HALF), 0) + m * MB
    at = pl.ds(pl.multiple_of(m * MB, MB), MB)
    for k in range(4):
        hot = jnp.where(goals[k : k + 1, :] == here, 1.0, 0.0).astype(jnp.bfloat16)
        total = dot_nt(chosen[...], hot).astype(jnp.bfloat16)
        for i in range(8):
            store((i, slice(k * VB, (k + 1) * VB), at), total[i * VB : (i + 1) * VB])


def protein_kernel(prot, perm, chosen, data, moved, goals, s_own, s1, r1, s2, r2, sa, ra, sb, rb, s3, r3, sd, rd):
    p, z, s = lax.axis_index("prot"), lax.axis_index("var"), lax.axis_index("samp")
    c, xh, y = p % 2, (p // 2) % 2, p // 4
    half, a = y // 2, (y % 2) * 2 + xh
    away = (s + half) % 2

    def device(y2, x2):
        return y2 * 4 + x2 * 2 + c

    barrier = pltpu.get_barrier_semaphore()

    def signal(dev):
        pl.semaphore_signal(barrier, inc=1, device_id=dev, device_id_type=MESH)

    source = device(2 * s + y // 2, y % 2)
    y_peers = [(device((y + d) % 4, xh), z, s) for d in (1, 2, 3)]
    up, down = (p, (z + 1) % 8, s), (p, (z + 7) % 8, s)
    sibling = (p + 1 - 2 * c, z, s)
    for dev in ((source, (z + 7) % 8, s), (source, (z + 7) % 8, 1 - s), *y_peers, up, down, sibling):
        signal(dev)
    goals[...] = (perm[...] + s * HALF) & (ALL - 1)
    pl.semaphore_wait(barrier, 8)

    def remote(src, dst, ssem, rsem, dev):
        return pltpu.make_async_remote_copy(
            src_ref=src, dst_ref=dst, send_sem=ssem, recv_sem=rsem, device_id=dev, device_id_type=MESH
        )

    def send(src, dst, ssem, rsem, dev):
        remote(src, dst, ssem, rsem, dev).start()

    def arrived(ref, rsem):
        remote(ref, ref, s_own, rsem, sibling).wait_recv()

    def left(ref, ssem):
        remote(ref, ref, ssem, s_own, sibling).wait_send()

    def lanes(z2, far=0):
        return pl.ds(pl.multiple_of(far * HALF + 128 * z2, 128), 128)

    def near(y2, z2):
        return data.at[y2, c, :, lanes(z2)]

    def near_all(z2):
        return data.at[:, c, :, lanes(z2)]

    def far(y2, z2):
        return data.at[y2, c, :, lanes(z2, 1)]

    def far_all(y2):
        return data.at[y2, c, :, pl.ds(HALF, HALF)]

    def pass_near(t, k):
        y2 = (y + 4 - k) % 4

        def go(way):
            here = near(y2, (z + (8 - t, t)[way]) % 8)
            send(here, here, sa.at[way, t, k], ra.at[way, t, k], (up, down)[way])

        go(k // 2)
        pl.when(t < 3)(lambda: go(1 - k // 2))

    def pass_far(t):
        here = far(y, (z + 8 - t) % 8)
        send(here, here, sb.at[0, t], rb.at[0, t], up)

        @pl.when(t < 3)
        def _():
            here = far(y, (z + t) % 8)
            send(here, here, sb.at[1, t], rb.at[1, t], down)

    def spread_far(dz):
        here = far(y, (z + dz) % 8)
        for d in (1, 2, 3):
            send(here, here, s3.at[d - 1, dz], r3.at[d - 1, dz], y_peers[d - 1])

    def share(ref, k):
        send(ref, ref, sd.at[k], rd.at[k], sibling)

    def ring(t):
        arrived(far(y, (z + 7 - t) % 8), rb.at[0, t])

        @pl.when(t < 3)
        def _():
            arrived(far(y, (z + 1 + t) % 8), rb.at[1, t])
            pass_far(t + 1)
            spread_far(1 + t)

        spread_far(7 - t)
        for k in range(4):
            y2 = (y + 4 - k) % 4
            way = k // 2
            arrived(near(y2, (z + (7 - t, 1 + t)[way]) % 8), ra.at[way, t, k])

            @pl.when(t < 3)
            def _():
                arrived(near(y2, (z + (1 + t, 7 - t)[way]) % 8), ra.at[1 - way, t, k])
                pass_near(t + 1, k)

        share(near_all((z + 7 - t) % 8), 1 + t)

        @pl.when(t < 3)
        def _():
            share(near_all((z + 1 + t) % 8), 5 + t)

    def step(n, _):
        @pl.when(n == 0)
        def _():
            z2 = (z + 1) % 8
            src, dst = prot.at[:, lanes(z2)], data.at[a, c, :, lanes(z2, away)]
            for x2 in range(2):
                send(src, dst, s1.at[x2], r1.at[away], (device(a, x2), z2, half))

        @pl.when(n == 1)
        def _():
            arrived(near(y, z), r1.at[0])
            for d in (1, 2, 3):
                send(near(y, z), near(y, z), s2.at[d - 1], r2.at[d - 1], y_peers[d - 1])
            pass_near(0, 0)
            arrived(far(y, z), r1.at[1])
            pass_far(0)
            spread_far(0)

        @pl.when(n == 2)
        def _():
            for d in (1, 2, 3):
                arrived(near((y + 4 - d) % 4, z), r2.at[d - 1])
                pass_near(0, d)
            share(near_all(z), 0)

        @pl.when((n >= 2) & (n < 6))
        def _():
            ring(n - 2)

        move_step(n, goals, chosen, lambda at, value: moved.__setitem__(at, value))
        return 0

    lax.fori_loop(0, ALL // MB, step, 0)
    share(far_all(y), 8)
    for d in (1, 2, 3):
        for dz in range(8):
            arrived(far((y + 4 - d) % 4, (z + dz) % 8), r3.at[d - 1, dz])
        share(far_all((y + 4 - d) % 4), 8 + d)

    def theirs_near(z2, k):
        arrived(data.at[:, 1 - c, :, lanes(z2)], rd.at[k])

    theirs_near(z, 0)
    for t in range(4):
        theirs_near((z + 7 - t) % 8, 1 + t)
        if t < 3:
            theirs_near((z + 1 + t) % 8, 5 + t)
    for d in range(4):
        arrived(data.at[(y + 4 - d) % 4, 1 - c, :, pl.ds(HALF, HALF)], rd.at[8 + d])

    one = near(y, z)
    for x2 in range(2):
        left(one, s1.at[x2])
    for d in range(3):
        left(one, s2.at[d])
        for dz in range(8):
            left(one, s3.at[d, dz])
    for t in range(4):
        for way in range(2 if t < 3 else 1):
            left(one, sb.at[way, t])
        for k in range(4):
            left(one, sa.at[k // 2, t, k])
            if t < 3:
                left(one, sa.at[1 - k // 2, t, k])
    for k in range(8):
        left(near_all(z), sd.at[k])
    for k in range(8, 12):
        left(far_all(y), sd.at[k])


def gather_proteins(prot, perm, chosen):
    dma = pltpu.SemaphoreType.DMA
    space, vmem = pl.BlockSpec(memory_space=pl.ANY), pl.BlockSpec(memory_space=pltpu.VMEM)
    return pl.pallas_call(
        protein_kernel,
        out_shape=[
            jax.ShapeDtypeStruct((4, 2, PB, ALL), jnp.bfloat16),
            jax.ShapeDtypeStruct((8, 4 * VB, ALL), jnp.bfloat16),
        ],
        in_specs=[space, vmem, vmem],
        out_specs=[space, vmem],
        scratch_shapes=[
            pltpu.VMEM((4, HALF), jnp.int32),
            dma, dma((2,)), dma((2,)), dma((3,)), dma((3,)), dma((2, 4, 4)), dma((2, 4, 4)),
            dma((2, 4)), dma((2, 4)), dma((3, 8)), dma((3, 8)), dma((12,)), dma((12,)),
        ],
        compiler_params=pltpu.CompilerParams(collective_id=1, has_side_effects=True, vmem_limit_bytes=18 * MIB),
        cost_estimate=pl.CostEstimate(flops=9_000_000_000, bytes_accessed=80 * MIB, transcendentals=0),
        name="gather_proteins",
    )(prot, perm, chosen)


def moments(a, b):
    a, b = a.astype(jnp.float32), b.astype(jnp.float32)
    mean = (jnp.sum(a, 1, keepdims=True) + jnp.sum(b, 1, keepdims=True)) / N
    var = (jnp.sum(a * a, 1, keepdims=True) + jnp.sum(b * b, 1, keepdims=True)) / N - mean * mean
    return mean, var


def scales(a, b):
    mean, var = moments(a, b)
    inv = jnp.sqrt(jnp.float32(N)) * lax.rsqrt(var + EPS)
    return inv / N, inv * mean


def as_rows(x, y):
    lane = lax.broadcasted_iota(jnp.int32, (x.shape[0], 128), 1)
    turned = jnp.transpose(jnp.where(lane == 0, x, y))
    return turned[0:1, :], turned[1:2, :]


def cis_kernel(plan, perm, prot, chosen_own, chosen, moved_own, out, stat, goals, moved, part, sums, near, every, s1, r1, s2, r2):
    p, z, s = lax.axis_index("prot"), lax.axis_index("var"), lax.axis_index("samp")
    barrier = pltpu.get_barrier_semaphore()

    def signal(dev):
        pl.semaphore_signal(barrier, inc=1, device_id=dev, device_id_type=MESH)

    for d in range(1, 8):
        signal((p, (z + d) % 8, s))
    home = p % 8
    at_home = 1 - ((z - home) * (z - home) + 63) // 64
    for d in range(16):
        signal((d, (home + at_home) % 8, p // 8))

    goals[...] = (perm[...] + s * HALF) & (ALL - 1)

    def store(at, value):
        moved[at] = moved_own[at] + value

    def move(m, _):
        move_step(m, goals, chosen, store)
        return 0

    lax.fori_loop(0, ALL // MB, move, 0)
    pl.semaphore_wait(barrier, 23)

    def remote(src, dst, ssem, rsem, dev):
        return pltpu.make_async_remote_copy(
            src_ref=src, dst_ref=dst, send_sem=ssem, recv_sem=rsem, device_id=dev, device_id_type=MESH
        )

    def block(n, _):
        i = (z + 1 + n) % 8
        mean, var = moments(prot[i, :, :HALF], prot[i, :, HALF:])
        inv = lax.rsqrt(var + EPS)
        stat[0, i] = jnp.broadcast_to(mean, (PB, 128))
        stat[1, i] = jnp.broadcast_to(inv, (PB, 128))
        mean, inv = as_rows(mean, inv)
        rows = pl.ds(pl.multiple_of(i * VB, VB), VB)
        by, off = scales(chosen_own[rows, :], chosen[rows, :])
        cross = dot_nt(moved[i], prot[i])
        keep = plan[PLAN_KEEP + i].astype(jnp.float32)
        for k in range(4):
            u = cross[k * VB : (k + 1) * VB] * by - off * mean
            part[i, k : k + 1, :PB] = jnp.sum(u * u, 0, keepdims=True) * (inv * inv) * keep

        @pl.when(n != 7)
        def _():
            remote(part.at[i], near.at[0, n], s1.at[0, n], r1.at[0, n], (p, i, s)).start()

        @pl.when(n != 6)
        def _():
            remote(part.at[i], near.at[1, n], s1.at[1, n], r1.at[1, n], (p, (i + 1) % 8, s)).start()

        return 0

    part[...] = jnp.zeros_like(part)
    lax.fori_loop(0, 8, block, 0)

    own_sends = []
    for side in range(2):
        total = part[(z + 8 - side) % 8]
        for n in range(8):
            if n != 7 - side:
                remote(part.at[0], near.at[side, n], s1.at[side, n], r1.at[side, n], (p, (z + 1) % 8, s)).wait_recv()
                total += near[side, n]
        sums[side] = total
        for ds in range(2):
            for dz in range(1, 8) if side == 0 else (7,):
                to = (8 * s + (z + 8 - side) % 8, (z + dz) % 8, (s + ds) % 2)
                copy = remote(sums.at[side], every.at[p], s2.at[side, ds, dz], r2.at[p], to)
                copy.start()
                own_sends.append(copy)
    total = jnp.zeros((4, 256), jnp.float32)
    for d in range(16):
        remote(sums.at[0], every.at[d], s2.at[0, 0, 0], r2.at[d], (p, (z + 1) % 8, s)).wait_recv()
        total += every[d]
    out[...] = total
    for copy in own_sends:
        copy.wait_send()
    for side in range(2):
        for n in range(8):
            if n != 7 - side:
                remote(part.at[0], near.at[side, n], s1.at[side, n], r1.at[side, n], (p, (z + 1) % 8, s)).wait_send()


def cis(plan, perm, prot, chosen_own, chosen_got, moved):
    smem, vmem = pl.BlockSpec(memory_space=pltpu.SMEM), pl.BlockSpec(memory_space=pltpu.VMEM)
    dma = pltpu.SemaphoreType.DMA
    return pl.pallas_call(
        cis_kernel,
        out_shape=[
            jax.ShapeDtypeStruct((4, 256), jnp.float32),
            jax.ShapeDtypeStruct((2, 8, PB, 128), jnp.float32),
        ],
        in_specs=[smem, *[vmem] * 5],
        out_specs=[vmem, vmem],
        scratch_shapes=[
            pltpu.VMEM((4, HALF), jnp.int32),
            pltpu.VMEM((8, 4 * VB, ALL), jnp.bfloat16),
            pltpu.VMEM((8, 4, 256), jnp.float32),
            pltpu.VMEM((2, 4, 256), jnp.float32),
            pltpu.VMEM((2, 8, 4, 256), jnp.float32),
            pltpu.VMEM((16, 4, 256), jnp.float32),
            dma((2, 8)), dma((2, 8)), dma((2, 2, 8)), dma((16,)),
        ],
        compiler_params=pltpu.CompilerParams(collective_id=2, has_side_effects=True, vmem_limit_bytes=30 * MIB),
        cost_estimate=pl.CostEstimate(flops=12_000_000_000, bytes_accessed=20 * MIB, transcendentals=0),
        name="cis",
    )(plan, perm, prot, chosen_own, chosen_got, moved)


def trans_kernel(chunks, first, last, aliased, plan, prot, stat, g_ref, *refs):
    got = refs[:chunks]
    out, rows, stage, sems = refs[chunks + aliased :]
    steps = (last - first) // 2

    def copy_out(n, h):
        column = pl.multiple_of(plan[PLAN_TILE + first + 2 * n + h] * 128, 128)
        return pltpu.make_async_copy(
            stage.at[n % 2, :, pl.ds(h * 128, 128)], out.at[:, pl.ds(column, 128)], sems.at[n % 2, h]
        )

    def step(n, _):
        for t in range(2):
            tile = plan[PLAN_TILE + first + 2 * n + t]
            at = t * 128
            rows[at : at + 128, :HALF] = g_ref[pl.ds(pl.multiple_of(tile * 128, 128), 128), :]
            for h in range(2):
                place = plan[tile * 2 + h]
                for c in range(chunks):

                    @pl.when((place >= STARTS[c]) & (place < STARTS[c] + CHUNKS[c]))
                    def _():
                        row = pl.multiple_of((place - STARTS[c]) * VB, VB)
                        rows[at + h * VB : at + (h + 1) * VB, HALF:] = got[c][pl.ds(row, VB), :]

        both = rows[...]
        by, off = as_rows(*scales(both[:, :HALF], both[:, HALF:]))
        cross = dot_nt(prot[...], both)
        mean = jnp.concatenate([stat[0], stat[0]], 1)
        inv = jnp.concatenate([stat[1], stat[1]], 1)

        @pl.when(n >= 2)
        def _():
            for h in range(2):
                copy_out(n - 2, h).wait()

        stage[n % 2] = ((cross * by - mean * off) * inv).astype(jnp.bfloat16)
        for h in range(2):
            copy_out(n, h).start()
        return 0

    lax.fori_loop(0, steps, step, 0)
    for n in range(max(steps - 2, 0), steps):
        for h in range(2):
            copy_out(n, h).wait()


def trans(chunks, first, last, plan, prot, stat, genotype, got, out):
    vmem, hbm = pl.BlockSpec(memory_space=pltpu.VMEM), pl.BlockSpec(memory_space=pltpu.HBM)
    operands = [plan, prot, stat, genotype, *got[:chunks]]
    specs = [pl.BlockSpec(memory_space=pltpu.SMEM), *[vmem] * (3 + chunks)]
    aliases = {}
    if out is not None:
        aliases = {len(operands): 0}
        operands.append(out)
        specs.append(hbm)
    return pl.pallas_call(
        functools.partial(trans_kernel, chunks, first, last, len(aliases)),
        out_shape=jax.ShapeDtypeStruct((COLS, ROWS), jnp.bfloat16),
        in_specs=specs,
        out_specs=hbm,
        scratch_shapes=[
            pltpu.VMEM((256, ALL), jnp.bfloat16),
            pltpu.VMEM((2, COLS, 256), jnp.bfloat16),
            pltpu.SemaphoreType.DMA((2, 2)),
        ],
        input_output_aliases=aliases,
        compiler_params=pltpu.CompilerParams(vmem_limit_bytes=20 * MIB),
        cost_estimate=pl.CostEstimate(
            flops=2 * COLS * ALL * 128 * (last - first), bytes_accessed=8 * MIB, transcendentals=0
        ),
        name="trans",
    )(*operands)


SWAP = [(0, 1), (1, 0)]


def body(genotype, proteins, cis_pick, perm_table):
    perm_got = lax.ppermute(perm_table, "samp", SWAP)
    mine, chosen, plan = sort_blocks(cis_pick, genotype)
    got = [lax.ppermute(chunk, "samp", SWAP) for chunk in mine]
    data, moved = gather_proteins(proteins.T, perm_table, chosen)
    prot = data.reshape(8, PB, ALL)
    total, stat = cis(plan, perm_got, prot, chosen, choose(plan, got[0]), moved)
    cis_stat = total[:, :PB] / jnp.float32(8 * HALF)
    out = None
    for chunks, first, last in GROUPS:
        out = trans(chunks, first, last, plan, prot.reshape(COLS, ALL), stat.reshape(2, COLS, 128), genotype, got, out)
    return out.T, cis_stat


def solution(mesh):
    return jax.shard_map(
        body,
        mesh=mesh,
        in_specs=(
            P(("prot", "var"), "samp"),
            P("samp", "prot"),
            P(("prot", "var"), None),
            P(None, "samp"),
        ),
        out_specs=(P(("prot", "var"), "samp"), P(None, "prot")),
        check_vma=False,
    )
```

```python
import functools

import jax
import jax.numpy as jnp
from jax import lax
from jax.experimental import pallas as pl
from jax.experimental.pallas import tpu as pltpu
from jax.sharding import PartitionSpec as P

MESH = pl.DeviceIdType.MESH
VB = 64
BLOCKS = 24
TILES = BLOCKS // 2
ROWS = VB * BLOCKS
HALF = 1024
ALL = 2 * HALF
PB = 184
COLS = 8 * PB
CHUNKS = (8, 16)
STARTS = tuple(sum(CHUNKS[:c]) for c in range(len(CHUNKS)))
GROUPS = ((2, 0, 12),)
EPS = 1e-6
N = float(ALL)
MIB = 1 << 20
NT = (((1,), (1,)), ((), ()))


def dot_nt(a, b):
    return lax.dot_general(a, b, NT, preferred_element_type=jnp.float32)


PLAN_TILE, PLAN_PLACE, PLAN_KEEP, PLAN = 24, 36, 44, 64


def block_order(pick_ref, first, flag, order):
    for b in range(BLOCKS):
        flag[b] = jnp.int32(0)
    for i in range(8):
        flag[pick_ref[0, first + i] & 31] = jnp.int32(1)
    flags = [flag[b] for b in range(BLOCKS)]
    at = jnp.int32(0)
    for rank in range(3):
        for b in range(BLOCKS):
            mine, pair = flags[b], flags[b ^ 1]
            order[at] = jnp.int32(b)
            at = at + (mine, (1 - mine) & pair, (1 - mine) & (1 - pair))[rank]


def sort_kernel(pick_ref, g_ref, *refs):
    outs, (chosen, plan, flag, order, seen) = refs[: len(CHUNKS)], refs[len(CHUNKS) :]
    samp = lax.axis_index("samp")
    block_order(pick_ref, 8 * (1 - samp), flag, order)
    for c, blocks in enumerate(CHUNKS):
        for t in range(blocks):
            row = pl.multiple_of(order[STARTS[c] + t] * VB, VB)
            outs[c][t * VB : (t + 1) * VB, :] = g_ref[pl.ds(row, VB), :]

    block_order(pick_ref, 8 * samp, flag, order)
    for t in range(TILES):
        seen[t] = jnp.int32(0)
    done = jnp.int32(0)
    for r in range(BLOCKS):
        b = order[r]
        plan[b] = jnp.int32(r)
        t = lax.shift_right_logical(b, 1)
        before = seen[t]
        seen[t] = before + 1
        plan[PLAN_TILE + done] = t
        done = done + before
    for i in range(8):
        pick = pick_ref[0, 8 * samp + i]
        keep = (pick >= 0).astype(jnp.int32)
        block = jnp.maximum(pick, 0)
        plan[PLAN_PLACE + i] = plan[block] * keep
        plan[PLAN_KEEP + i] = keep
        chosen[i * VB : (i + 1) * VB, :] = g_ref[pl.ds(pl.multiple_of(block * VB, VB), VB), :]


def sort_blocks(pick, genotype):
    smem, vmem = pl.BlockSpec(memory_space=pltpu.SMEM), pl.BlockSpec(memory_space=pltpu.VMEM)
    *mine, chosen, plan = pl.pallas_call(
        sort_kernel,
        out_shape=[
            *[jax.ShapeDtypeStruct((b * VB, HALF), jnp.bfloat16) for b in CHUNKS],
            jax.ShapeDtypeStruct((8 * VB, HALF), jnp.bfloat16),
            jax.ShapeDtypeStruct((PLAN,), jnp.int32),
        ],
        in_specs=[smem, vmem],
        out_specs=[vmem] * (len(CHUNKS) + 1) + [smem],
        scratch_shapes=[pltpu.SMEM((n,), jnp.int32) for n in (32, 32, TILES)],
        compiler_params=pltpu.CompilerParams(vmem_limit_bytes=14 * MIB),
        name="sort_blocks",
    )(pick, genotype)
    return mine, chosen, plan


def choose_kernel(plan, got, chosen):
    for i in range(8):
        row = pl.multiple_of(plan[PLAN_PLACE + i] * VB, VB)
        chosen[i * VB : (i + 1) * VB, :] = got[pl.ds(row, VB), :]


def choose(plan, got):
    vmem = pl.BlockSpec(memory_space=pltpu.VMEM)
    return pl.pallas_call(
        choose_kernel,
        out_shape=jax.ShapeDtypeStruct((8 * VB, HALF), jnp.bfloat16),
        in_specs=[pl.BlockSpec(memory_space=pltpu.SMEM), vmem],
        out_specs=vmem,
        compiler_params=pltpu.CompilerParams(vmem_limit_bytes=4 * MIB),
        name="choose",
    )(plan, got)


MB = 256


def move_step(m, goals, chosen, store):
    here = lax.broadcasted_iota(jnp.int32, (MB, HALF), 0) + m * MB
    at = pl.ds(pl.multiple_of(m * MB, MB), MB)
    for k in range(4):
        hot = jnp.where(goals[k : k + 1, :] == here, 1.0, 0.0).astype(jnp.bfloat16)
        total = dot_nt(chosen[...], hot).astype(jnp.bfloat16)
        for i in range(8):
            store((i, slice(k * VB, (k + 1) * VB), at), total[i * VB : (i + 1) * VB])


def protein_kernel(prot, perm, chosen, data, moved, goals, s_own, s1, r1, s2, r2, sa, ra, sb, rb, s3, r3, sd, rd):
    p, z, s = lax.axis_index("prot"), lax.axis_index("var"), lax.axis_index("samp")
    c, xh, y = p % 2, (p // 2) % 2, p // 4
    half, a = y // 2, (y % 2) * 2 + xh
    away = (s + half) % 2

    def device(y2, x2):
        return y2 * 4 + x2 * 2 + c

    barrier = pltpu.get_barrier_semaphore()

    def signal(dev):
        pl.semaphore_signal(barrier, inc=1, device_id=dev, device_id_type=MESH)

    source = device(2 * s + y // 2, y % 2)
    y_peers = [(device((y + d) % 4, xh), z, s) for d in (1, 2, 3)]
    up, down = (p, (z + 1) % 8, s), (p, (z + 7) % 8, s)
    sibling = (p + 1 - 2 * c, z, s)
    for dev in ((source, (z + 7) % 8, s), (source, (z + 7) % 8, 1 - s), *y_peers, up, down, sibling):
        signal(dev)
    goals[...] = (perm[...] + s * HALF) & (ALL - 1)
    pl.semaphore_wait(barrier, 8)

    def remote(src, dst, ssem, rsem, dev):
        return pltpu.make_async_remote_copy(
            src_ref=src, dst_ref=dst, send_sem=ssem, recv_sem=rsem, device_id=dev, device_id_type=MESH
        )

    def send(src, dst, ssem, rsem, dev):
        remote(src, dst, ssem, rsem, dev).start()

    def arrived(ref, rsem):
        remote(ref, ref, s_own, rsem, sibling).wait_recv()

    def left(ref, ssem):
        remote(ref, ref, ssem, s_own, sibling).wait_send()

    def lanes(z2, far=0):
        return pl.ds(pl.multiple_of(far * HALF + 128 * z2, 128), 128)

    def near(y2, z2):
        return data.at[y2, c, :, lanes(z2)]

    def near_all(z2):
        return data.at[:, c, :, lanes(z2)]

    def far(y2, z2):
        return data.at[y2, c, :, lanes(z2, 1)]

    def far_all(y2):
        return data.at[y2, c, :, pl.ds(HALF, HALF)]

    def pass_near(t, k):
        y2 = (y + 4 - k) % 4

        def go(way):
            here = near(y2, (z + (8 - t, t)[way]) % 8)
            send(here, here, sa.at[way, t, k], ra.at[way, t, k], (up, down)[way])

        go(k // 2)
        pl.when(t < 3)(lambda: go(1 - k // 2))

    def pass_far(t):
        here = far(y, (z + 8 - t) % 8)
        send(here, here, sb.at[0, t], rb.at[0, t], up)

        @pl.when(t < 3)
        def _():
            here = far(y, (z + t) % 8)
            send(here, here, sb.at[1, t], rb.at[1, t], down)

    def spread_far(dz):
        here = far(y, (z + dz) % 8)
        for d in (1, 2, 3):
            send(here, here, s3.at[d - 1, dz], r3.at[d - 1, dz], y_peers[d - 1])

    def share(ref, k):
        send(ref, ref, sd.at[k], rd.at[k], sibling)

    def ring(t):
        arrived(far(y, (z + 7 - t) % 8), rb.at[0, t])

        @pl.when(t < 3)
        def _():
            arrived(far(y, (z + 1 + t) % 8), rb.at[1, t])
            pass_far(t + 1)
            spread_far(1 + t)

        spread_far(7 - t)
        for k in range(4):
            y2 = (y + 4 - k) % 4
            way = k // 2
            arrived(near(y2, (z + (7 - t, 1 + t)[way]) % 8), ra.at[way, t, k])

            @pl.when(t < 3)
            def _():
                arrived(near(y2, (z + (1 + t, 7 - t)[way]) % 8), ra.at[1 - way, t, k])
                pass_near(t + 1, k)

        share(near_all((z + 7 - t) % 8), 1 + t)

        @pl.when(t < 3)
        def _():
            share(near_all((z + 1 + t) % 8), 5 + t)

    def step(n, _):
        @pl.when(n == 0)
        def _():
            z2 = (z + 1) % 8
            src, dst = prot.at[:, lanes(z2)], data.at[a, c, :, lanes(z2, away)]
            for x2 in range(2):
                send(src, dst, s1.at[x2], r1.at[away], (device(a, x2), z2, half))

        @pl.when(n == 1)
        def _():
            arrived(near(y, z), r1.at[0])
            for d in (1, 2, 3):
                send(near(y, z), near(y, z), s2.at[d - 1], r2.at[d - 1], y_peers[d - 1])
            pass_near(0, 0)
            arrived(far(y, z), r1.at[1])
            pass_far(0)
            spread_far(0)

        @pl.when(n == 2)
        def _():
            for d in (1, 2, 3):
                arrived(near((y + 4 - d) % 4, z), r2.at[d - 1])
                pass_near(0, d)
            share(near_all(z), 0)

        @pl.when((n >= 2) & (n < 6))
        def _():
            ring(n - 2)

        move_step(n, goals, chosen, lambda at, value: moved.__setitem__(at, value))
        return 0

    lax.fori_loop(0, ALL // MB, step, 0)
    share(far_all(y), 8)
    for d in (1, 2, 3):
        for dz in range(8):
            arrived(far((y + 4 - d) % 4, (z + dz) % 8), r3.at[d - 1, dz])
        share(far_all((y + 4 - d) % 4), 8 + d)

    def theirs_near(z2, k):
        arrived(data.at[:, 1 - c, :, lanes(z2)], rd.at[k])

    theirs_near(z, 0)
    for t in range(4):
        theirs_near((z + 7 - t) % 8, 1 + t)
        if t < 3:
            theirs_near((z + 1 + t) % 8, 5 + t)
    for d in range(4):
        arrived(data.at[(y + 4 - d) % 4, 1 - c, :, pl.ds(HALF, HALF)], rd.at[8 + d])

    one = near(y, z)
    for x2 in range(2):
        left(one, s1.at[x2])
    for d in range(3):
        left(one, s2.at[d])
        for dz in range(8):
            left(one, s3.at[d, dz])
    for t in range(4):
        for way in range(2 if t < 3 else 1):
            left(one, sb.at[way, t])
        for k in range(4):
            left(one, sa.at[k // 2, t, k])
            if t < 3:
                left(one, sa.at[1 - k // 2, t, k])
    for k in range(8):
        left(near_all(z), sd.at[k])
    for k in range(8, 12):
        left(far_all(y), sd.at[k])


def gather_proteins(prot, perm, chosen):
    dma = pltpu.SemaphoreType.DMA
    space, vmem = pl.BlockSpec(memory_space=pl.ANY), pl.BlockSpec(memory_space=pltpu.VMEM)
    return pl.pallas_call(
        protein_kernel,
        out_shape=[
            jax.ShapeDtypeStruct((4, 2, PB, ALL), jnp.bfloat16),
            jax.ShapeDtypeStruct((8, 4 * VB, ALL), jnp.bfloat16),
        ],
        in_specs=[space, vmem, vmem],
        out_specs=[space, vmem],
        scratch_shapes=[
            pltpu.VMEM((4, HALF), jnp.int32),
            dma, dma((2,)), dma((2,)), dma((3,)), dma((3,)), dma((2, 4, 4)), dma((2, 4, 4)),
            dma((2, 4)), dma((2, 4)), dma((3, 8)), dma((3, 8)), dma((12,)), dma((12,)),
        ],
        compiler_params=pltpu.CompilerParams(collective_id=1, has_side_effects=True, vmem_limit_bytes=18 * MIB),
        cost_estimate=pl.CostEstimate(flops=9_000_000_000, bytes_accessed=80 * MIB, transcendentals=0),
        name="gather_proteins",
    )(prot, perm, chosen)


def moments(a, b):
    a, b = a.astype(jnp.float32), b.astype(jnp.float32)
    mean = (jnp.sum(a, 1, keepdims=True) + jnp.sum(b, 1, keepdims=True)) / N
    var = (jnp.sum(a * a, 1, keepdims=True) + jnp.sum(b * b, 1, keepdims=True)) / N - mean * mean
    return mean, var


def scales(a, b):
    mean, var = moments(a, b)
    inv = jnp.sqrt(jnp.float32(N)) * lax.rsqrt(var + EPS)
    return inv / N, inv * mean


def as_rows(x, y):
    lane = lax.broadcasted_iota(jnp.int32, (x.shape[0], 128), 1)
    turned = jnp.transpose(jnp.where(lane == 0, x, y))
    return turned[0:1, :], turned[1:2, :]


def cis_kernel(plan, perm, prot, chosen_own, chosen, moved_own, out, stat, goals, moved, part, sums, near, every, s1, r1, s2, r2):
    p, z, s = lax.axis_index("prot"), lax.axis_index("var"), lax.axis_index("samp")
    barrier = pltpu.get_barrier_semaphore()

    def signal(dev):
        pl.semaphore_signal(barrier, inc=1, device_id=dev, device_id_type=MESH)

    for d in range(1, 8):
        signal((p, (z + d) % 8, s))
    home = p % 8
    at_home = 1 - ((z - home) * (z - home) + 63) // 64
    for d in range(16):
        signal((d, (home + at_home) % 8, p // 8))

    goals[...] = (perm[...] + s * HALF) & (ALL - 1)

    def store(at, value):
        moved[at] = moved_own[at] + value

    def move(m, _):
        move_step(m, goals, chosen, store)
        return 0

    lax.fori_loop(0, ALL // MB, move, 0)
    pl.semaphore_wait(barrier, 23)

    def remote(src, dst, ssem, rsem, dev):
        return pltpu.make_async_remote_copy(
            src_ref=src, dst_ref=dst, send_sem=ssem, recv_sem=rsem, device_id=dev, device_id_type=MESH
        )

    def block(n, _):
        i = (z + 1 + n) % 8
        mean, var = moments(prot[i, :, :HALF], prot[i, :, HALF:])
        inv = lax.rsqrt(var + EPS)
        stat[0, i] = jnp.broadcast_to(mean, (PB, 128))
        stat[1, i] = jnp.broadcast_to(inv, (PB, 128))
        mean, inv = as_rows(mean, inv)
        rows = pl.ds(pl.multiple_of(i * VB, VB), VB)
        by, off = scales(chosen_own[rows, :], chosen[rows, :])
        cross = dot_nt(moved[i], prot[i])
        keep = plan[PLAN_KEEP + i].astype(jnp.float32)
        for k in range(4):
            u = cross[k * VB : (k + 1) * VB] * by - off * mean
            part[i, k : k + 1, :PB] = jnp.sum(u * u, 0, keepdims=True) * (inv * inv) * keep

        @pl.when(n != 7)
        def _():
            remote(part.at[i], near.at[0, n], s1.at[0, n], r1.at[0, n], (p, i, s)).start()

        @pl.when(n != 6)
        def _():
            remote(part.at[i], near.at[1, n], s1.at[1, n], r1.at[1, n], (p, (i + 1) % 8, s)).start()

        return 0

    part[...] = jnp.zeros_like(part)
    lax.fori_loop(0, 8, block, 0)

    own_sends = []
    for side in range(2):
        total = part[(z + 8 - side) % 8]
        for n in range(8):
            if n != 7 - side:
                remote(part.at[0], near.at[side, n], s1.at[side, n], r1.at[side, n], (p, (z + 1) % 8, s)).wait_recv()
                total += near[side, n]
        sums[side] = total
        for ds in range(2):
            for dz in range(1, 8) if side == 0 else (7,):
                to = (8 * s + (z + 8 - side) % 8, (z + dz) % 8, (s + ds) % 2)
                copy = remote(sums.at[side], every.at[p], s2.at[side, ds, dz], r2.at[p], to)
                copy.start()
                own_sends.append(copy)
    total = jnp.zeros((4, 256), jnp.float32)
    for d in range(16):
        remote(sums.at[0], every.at[d], s2.at[0, 0, 0], r2.at[d], (p, (z + 1) % 8, s)).wait_recv()
        total += every[d]
    out[...] = total
    for copy in own_sends:
        copy.wait_send()
    for side in range(2):
        for n in range(8):
            if n != 7 - side:
                remote(part.at[0], near.at[side, n], s1.at[side, n], r1.at[side, n], (p, (z + 1) % 8, s)).wait_send()


def cis(plan, perm, prot, chosen_own, chosen_got, moved):
    smem, vmem = pl.BlockSpec(memory_space=pltpu.SMEM), pl.BlockSpec(memory_space=pltpu.VMEM)
    dma = pltpu.SemaphoreType.DMA
    return pl.pallas_call(
        cis_kernel,
        out_shape=[
            jax.ShapeDtypeStruct((4, 256), jnp.float32),
            jax.ShapeDtypeStruct((2, 8, PB, 128), jnp.float32),
        ],
        in_specs=[smem, *[vmem] * 5],
        out_specs=[vmem, vmem],
        scratch_shapes=[
            pltpu.VMEM((4, HALF), jnp.int32),
            pltpu.VMEM((8, 4 * VB, ALL), jnp.bfloat16),
            pltpu.VMEM((8, 4, 256), jnp.float32),
            pltpu.VMEM((2, 4, 256), jnp.float32),
            pltpu.VMEM((2, 8, 4, 256), jnp.float32),
            pltpu.VMEM((16, 4, 256), jnp.float32),
            dma((2, 8)), dma((2, 8)), dma((2, 2, 8)), dma((16,)),
        ],
        compiler_params=pltpu.CompilerParams(collective_id=2, has_side_effects=True, vmem_limit_bytes=30 * MIB),
        cost_estimate=pl.CostEstimate(flops=12_000_000_000, bytes_accessed=20 * MIB, transcendentals=0),
        name="cis",
    )(plan, perm, prot, chosen_own, chosen_got, moved)


def trans_kernel(chunks, first, last, aliased, plan, prot, stat, g_ref, *refs):
    got = refs[:chunks]
    out, rows, halves, stage, sems = refs[chunks + aliased :]
    for c in range(chunks):
        halves[STARTS[c] * VB : (STARTS[c] + CHUNKS[c]) * VB, :] = got[c][...]
    steps = (last - first) // 2

    def copy_out(n, h):
        column = pl.multiple_of(plan[PLAN_TILE + first + 2 * n + h] * 128, 128)
        return pltpu.make_async_copy(
            stage.at[n % 2, :, pl.ds(h * 128, 128)], out.at[:, pl.ds(column, 128)], sems.at[n % 2, h]
        )

    def step(n, _):
        @pl.when(n >= 2)
        def _():
            for h in range(2):
                copy_out(n - 2, h).wait()

        for t in range(2):
            tile = plan[PLAN_TILE + first + 2 * n + t]
            at = t * 128
            rows[at : at + 128, :HALF] = g_ref[pl.ds(pl.multiple_of(tile * 128, 128), 128), :]
            for h in range(2):
                row = pl.multiple_of(plan[tile * 2 + h] * VB, VB)
                rows[at + h * VB : at + (h + 1) * VB, HALF:] = halves[pl.ds(row, VB), :]

        both = rows[...]
        by, off = as_rows(*scales(both[:, :HALF], both[:, HALF:]))
        cross = dot_nt(prot[...], both)
        mean = jnp.concatenate([stat[0], stat[0]], 1)
        inv = jnp.concatenate([stat[1], stat[1]], 1)
        stage[n % 2] = ((cross * by - mean * off) * inv).astype(jnp.bfloat16)
        for h in range(2):
            copy_out(n, h).start()
        return 0

    lax.fori_loop(0, steps, step, 0)
    for n in range(max(steps - 2, 0), steps):
        for h in range(2):
            copy_out(n, h).wait()


def trans(chunks, first, last, plan, prot, stat, genotype, got, out):
    vmem, hbm = pl.BlockSpec(memory_space=pltpu.VMEM), pl.BlockSpec(memory_space=pltpu.HBM)
    operands = [plan, prot, stat, genotype, *got[:chunks]]
    specs = [pl.BlockSpec(memory_space=pltpu.SMEM), *[vmem] * (3 + chunks)]
    aliases = {}
    if out is not None:
        aliases = {len(operands): 0}
        operands.append(out)
        specs.append(hbm)
    return pl.pallas_call(
        functools.partial(trans_kernel, chunks, first, last, len(aliases)),
        out_shape=jax.ShapeDtypeStruct((COLS, ROWS), jnp.bfloat16),
        in_specs=specs,
        out_specs=hbm,
        scratch_shapes=[
            pltpu.VMEM((256, ALL), jnp.bfloat16),
            pltpu.VMEM((ROWS, HALF), jnp.bfloat16),
            pltpu.VMEM((2, COLS, 256), jnp.bfloat16),
            pltpu.SemaphoreType.DMA((2, 2)),
        ],
        input_output_aliases=aliases,
        compiler_params=pltpu.CompilerParams(vmem_limit_bytes=20 * MIB),
        cost_estimate=pl.CostEstimate(
            flops=2 * COLS * ALL * 128 * (last - first), bytes_accessed=8 * MIB, transcendentals=0
        ),
        name="trans",
    )(*operands)


SWAP = [(0, 1), (1, 0)]


def body(genotype, proteins, cis_pick, perm_table):
    perm_got = lax.ppermute(perm_table, "samp", SWAP)
    mine, chosen, plan = sort_blocks(cis_pick, genotype)
    got = [lax.ppermute(chunk, "samp", SWAP) for chunk in mine]
    data, moved = gather_proteins(proteins.T, perm_table, chosen)
    prot = data.reshape(8, PB, ALL)
    total, stat = cis(plan, perm_got, prot, chosen, choose(plan, got[0]), moved)
    cis_stat = total[:, :PB] / jnp.float32(8 * HALF)
    out = None
    for chunks, first, last in GROUPS:
        out = trans(chunks, first, last, plan, prot.reshape(COLS, ALL), stat.reshape(2, COLS, 128), genotype, got, out)
    return out.T, cis_stat


def solution(mesh):
    return jax.shard_map(
        body,
        mesh=mesh,
        in_specs=(
            P(("prot", "var"), "samp"),
            P("samp", "prot"),
            P(("prot", "var"), None),
            P(None, "samp"),
        ),
        out_specs=(P(("prot", "var"), "samp"), P(None, "prot")),
        check_vma=False,
    )
```
